32 devices in a mesh: row: 4 (over y, x), sim: 8 (over z, core).
Axes of the slice: x: 2, y: 2, z: 4, core: 2. Of those that a mesh axis runs over, the one named last changes fastest.
Arguments:
- right_side: float32 [6144, 10240], P('row', 'sim'), may hold values from -6 to 6
- lower_panels: float32 [3, 6144, 512], P(None, ('row', 'sim')), may hold values from -0.15625 to 0.15625
- inverse_blocks: float32 [3, 512, 512], replicated, may hold values from -1 to 1.5, as said below
Outputs:
- solved: float32 [1536, 10240], P('row', 'sim')
- updated: float32 [6144, 10240], P('row', 'sim')
The draws below stay inside these ranges and needn't reach their ends.
Inputs may be any that keep to these rules, and one draw needn't show every extreme that they name: `inverse_blocks`: each block is lower triangular with a diagonal between 0.5 and 1.5.
All inputs are finite; a program needn't handle non-finite values.
Results may differ from the reference program's by a relative error of at most 0.0001.
Values sent between devices are 32-bit elements; how exact they have to be, the bound alone decides.
A program may use at most 128 MiB of HBM per device.

```python
import jax
import jax.numpy as jnp
from jax import lax

NB = 512
PANELS = 3
BLK_DEV = 3
BLOCKS = 12
SIMS = 10240
N_ROW = 4


def draw_inverse_blocks(key, part):
    first_key, second_key = jax.random.split(jax.random.fold_in(key, 17))
    noise = jnp.clip(jax.random.normal(first_key, (PANELS, NB, NB), jnp.float32), -4.0, 4.0) * (0.5 * NB ** (-0.5))
    diagonal = jax.random.uniform(second_key, (PANELS, NB), jnp.float32, 0.5, 1.5)
    strict = jnp.tril(jnp.ones((NB, NB), jnp.float32), -1)
    identity = jnp.eye(NB, dtype=jnp.float32)
    return noise * strict[None] + diagonal[:, None, :] * identity[None]


def block_scale(stream_key, extent, cuts, least, largest):
    loudness, own = 1.0, jax.random.fold_in(stream_key, 6)
    for position, parts in cuts:
        steps = jnp.exp(jax.random.uniform(jax.random.fold_in(own, position), (parts,), jnp.float32, least / len(cuts), largest / len(cuts)))
        loudness = loudness * jnp.repeat(steps, extent[position] // parts).reshape([-1 if axis == position else 1 for axis in range(len(extent))])
    return loudness


def centred(rng, extent, spread, bound, pieces=(), kind=jnp.bfloat16):
    array = spread * jax.random.normal(rng, extent, jnp.float32)
    if pieces:
        array = array * block_scale(rng, extent, pieces, -0.22, 0.18)
    return jnp.clip(array, -bound, bound).astype(kind)


def setup_inputs(seed: int = 0) -> dict:
    keys = jax.random.split(jax.random.key(seed), 4)
    right_side = centred(keys[0], (BLOCKS * NB, SIMS), 1.0, 6.0, ((0, 4), (1, 8)), jnp.float32)
    lower_panels = centred(keys[1], (PANELS, BLOCKS * NB, NB), (PANELS * NB) ** -0.5, 0.15625, ((1, 32),), jnp.float32)
    inverse_blocks = draw_inverse_blocks(jax.random.fold_in(keys[3], 71), 0)
    return {"right_side": right_side, "lower_panels": lower_panels, "inverse_blocks": inverse_blocks}


def reference(right_side, lower_panels, inverse_blocks):
    sims = right_side.shape[1]
    block_total = BLK_DEV * N_ROW
    blocks = right_side.reshape(N_ROW, BLK_DEV, NB, sims).transpose(1, 0, 2, 3).reshape(block_total, NB, sims)
    factor = lower_panels.reshape(PANELS, N_ROW, BLK_DEV, NB, NB).transpose(0, 2, 1, 3, 4).reshape(PANELS, block_total, NB, NB)
    order = jnp.arange(block_total)
    solved_list = []
    for panel in range(PANELS):
        solved_block = jnp.dot(inverse_blocks[panel], blocks[panel], precision=lax.Precision.HIGHEST, preferred_element_type=jnp.float32)
        solved_list.append(solved_block)
        change = jnp.einsum("bij,jn->bin", factor[panel], solved_block, precision=lax.Precision.HIGHEST)
        keeping = (order > panel).astype(jnp.float32)[:, None, None]
        blocks = blocks - keeping * change
    updated = blocks.reshape(BLK_DEV, N_ROW, NB, sims).transpose(1, 0, 2, 3).reshape(N_ROW * BLK_DEV * NB, sims)
    return jnp.concatenate(solved_list, 0), updated
```

```python
import functools
import math

import jax
import jax.numpy as jnp
from jax import lax
from jax.experimental import pallas as pl
from jax.experimental.pallas import tpu as pltpu
from jax.sharding import PartitionSpec as P

MESH = pl.DeviceIdType.MESH
CHUNK = 256
TILE = 256


def split(x):
    high = x.astype(jnp.bfloat16)
    return high, (x - high.astype(jnp.float32)).astype(jnp.bfloat16)


def mul(a, b):
    return jnp.dot(a, b, preferred_element_type=jnp.float32)


def ring_position(row, rows):
    return row // 2 if row % 2 == 0 else rows - 1 - row // 2


def kernel(R, S, b_hbm, l_hbm, inv_hbm, solved_hbm, upd_hbm, bv, lg, lh, ll, yv, yh, yl, iv, ih, il,
           lrecv, lsend, lown, yrecv, ysend, bsem, isem, osem, ssem):
    panels, chunks, nb, width = yv.shape
    rows = bv.shape[1]
    h = lg.shape[2]
    Z = S // 2
    r, s = lax.axis_index("row"), lax.axis_index("sim")
    z, core = s // 2, s % 2
    partner = s + 1 - 2 * core
    half = R // 2
    pos = jnp.where(r % 2 == 0, r // 2, R - 1 - r // 2)

    def row_at(position):
        q = lax.rem(position + R, R)
        return jnp.where(q < half, 2 * q, 2 * (R - 1 - q) + 1)

    right, left = row_at(pos + 1), row_at(pos - 1)
    up, down = lax.rem(s + 2, S), lax.rem(s + S - 2, S)

    barrier = pltpu.get_barrier_semaphore()
    for target in ((right, s), (left, s), (r, up), (r, down), (r, partner)):
        pl.semaphore_signal(barrier, inc=1, device_id=target, device_id_type=MESH)

    own_copies = [pltpu.make_async_copy(l_hbm.at[p], lg.at[p, s], lown.at[p]) for p in range(panels)]
    solver = r < panels
    inv_copy = pltpu.make_async_copy(inv_hbm.at[jnp.minimum(r, panels - 1)], iv, isem)
    inv_copy.start()
    b_copies = [
        pltpu.make_async_copy(b_hbm.at[:, pl.ds(c * width, width)], bv.at[c], bsem.at[c]) for c in range(chunks)
    ]
    b_copies[0].start()
    for copy in own_copies:
        copy.start()
    for copy in b_copies[1:]:
        copy.start()
    pl.semaphore_wait(barrier, 5)

    pending = []

    def send(cond, make):
        @pl.when(cond)
        def _():
            make().start()

        pending.append((cond, make))

    def l_copy(p, slot, way, target, own):
        src = l_hbm.at[p] if own else lg.at[p, slot]
        return pltpu.make_async_remote_copy(
            src_ref=src, dst_ref=lg.at[p, slot], send_sem=lsend.at[way, p, slot], recv_sem=lrecv.at[p, slot],
            device_id=(r, target), device_id_type=MESH,
        )

    def l_up(p, zz):
        slot = 2 * zz + core
        send(z == zz, lambda: l_copy(p, slot, 0, up, True))

        @pl.when(z > zz)
        def _():
            l_copy(p, slot, 0, up, False).wait_recv()

        send((z > zz) & (z < Z - 1), lambda: l_copy(p, slot, 0, up, False))
        send(z > zz, lambda: l_copy(p, slot, 2, partner, False))

    def l_down(p, zz):
        slot = 2 * zz + core
        send(z == zz, lambda: l_copy(p, slot, 1, down, True))

        @pl.when(z < zz)
        def _():
            l_copy(p, slot, 1, down, False).wait_recv()

        send((z < zz) & (z > 0), lambda: l_copy(p, slot, 1, down, False))
        send(z < zz, lambda: l_copy(p, slot, 2, partner, False))

    own_waited = set()

    def convert(p, zz):
        if p not in own_waited:
            own_waited.add(p)
            own_copies[p].wait()
        l_copy(p, 2 * zz + 1 - core, 2, partner, False).wait_recv()
        for k in range(2):
            first = (2 * zz + k) * h
            value = lg[p, 2 * zz + k]
            if first // nb * R <= p:
                row = first + lax.broadcasted_iota(jnp.int32, (h, 1), 0)
                block = jnp.where(row < nb * (first // nb + 1), first // nb, first // nb + 1) * R + r
                value = jnp.where(block > p, value, 0.0)
            high, low = split(value)
            lh[p, first:first + h] = high
            ll[p, first:first + h] = low

    lead = min(Z, -(-nb // (2 * h)))
    ups = [(panels - 1, zz) for zz in range(lead, Z - 1)]
    ups += [(p, zz) for p in range(panels - 1) for zz in range(min(lead, Z - 1))]
    ups += [(p, zz) for p in range(panels) for zz in reversed(range(Z - 1)) if (p, zz) not in ups]
    downs = [(p, zz) for p in range(panels - 1) for zz in range(1, lead)]
    downs += [(p, zz) for p in range(panels) for zz in range(1, Z) if (p, zz) not in downs]
    state = {"next": 0}
    seen_up, seen_down, converted = set(), set(), set()

    def l_step():
        i = state["next"]
        if i >= len(ups):
            return
        state["next"] += 1
        l_up(*ups[i])
        l_down(*downs[i])
        seen_up.add(ups[i])
        seen_down.add(downs[i])

    def l_convert():
        for p in range(panels):
            for zz in range(Z):
                ready = ((p, zz) in seen_up or zz == Z - 1) and ((p, zz) in seen_down or zz == 0)
                if ready and (p, zz) not in converted:
                    converted.add((p, zz))
                    convert(p, zz)

    def l_need(p, count):
        while not all(((p, zz) in seen_up or zz == Z - 1) and ((p, zz) in seen_down or zz == 0) for zz in range(count)):
            l_step()
        l_convert()

    def y_copy(k, c, way, target):
        return pltpu.make_async_remote_copy(
            src_ref=yv.at[k, c], dst_ref=yv.at[k, c], send_sem=ysend.at[way, k, c], recv_sem=yrecv.at[k, c],
            device_id=(target, s), device_id_type=MESH,
        )

    def reach(k, c):
        if k == 0:
            rightward = half if 5 * c < 3 * chunks else half - 1
        else:
            rightward = half - 1 if k == 1 else half
        return rightward, R - 1 - rightward

    def distance(k):
        return lax.rem(pos - ring_position(k, R) + R, R)

    def y_make(k, c):
        @pl.when(r == k)
        def _():
            high, low = split(bv[c, 0:nb])

            def body(i, carry):
                rows_i = pl.ds(pl.multiple_of(i * TILE, TILE), TILE)
                value = mul(ih[rows_i], high) + mul(ih[rows_i], low) + mul(il[rows_i], high)
                yv[k, c, rows_i] = value
                top, rest = split(value)
                yh[k, c, rows_i] = top
                yl[k, c, rows_i] = rest
                return carry

            lax.fori_loop(0, nb // TILE, body, 0)

        send(r == k, lambda: y_copy(k, c, 0, right))
        if reach(k, c)[1] > 0:
            send(r == k, lambda: y_copy(k, c, 1, left))

    def y_recv(k, c):
        @pl.when(r != k)
        def _():
            y_copy(k, c, 0, right).wait_recv()

        d = distance(k)
        rightward, leftward = reach(k, c)
        if rightward > 1:
            send((d > 0) & (d < rightward), lambda: y_copy(k, c, 0, right))
        if leftward > 1:
            send((d > 0) & (R - d < leftward), lambda: y_copy(k, c, 1, left))

        @pl.when(r != k)
        def _():
            top, rest = split(yv[k, c])
            yh[k, c] = top
            yl[k, c] = rest

    def update(ps, c, start, count):
        def body(i, carry):
            rows_i = pl.ds(pl.multiple_of(start + i * TILE, TILE), TILE)
            total = None
            for p in ps:
                part = mul(lh[p, rows_i], yh[p, c]) + mul(lh[p, rows_i], yl[p, c]) + mul(ll[p, rows_i], yh[p, c])
                total = part if total is None else total + part
            bv[c, rows_i] = bv[c, rows_i] - total
            return carry

        lax.fori_loop(0, count // TILE, body, 0)

    def y_lead(k, c):
        @pl.when(r > k)
        def _():
            update((k,), c, 0, nb)

    def rest(ps, c):
        update(ps, c, nb, rows - nb)

    outs = []

    def write(c):
        copy = pltpu.make_async_copy(bv.at[c], upd_hbm.at[:, pl.ds(c * width, width)], osem.at[c])
        copy.start()
        outs.append(copy)
        share = solved_hbm.shape[0]
        piece = math.gcd(share, nb)
        for i in range(share // piece):
            q = r * share + i * piece
            source = yv.at[q // nb, c, pl.ds(pl.multiple_of(q % nb, piece), piece)]
            copy = pltpu.make_async_copy(
                source, solved_hbm.at[pl.ds(i * piece, piece), pl.ds(c * width, width)], ssem.at[i, c]
            )
            copy.start()
            outs.append(copy)

    for p in range(panels):
        send(z >= 0, lambda p=p: l_copy(p, s, 2, partner, True))
    l_step()
    inv_copy.wait()

    @pl.when(solver)
    def _():
        high, low = split(iv[...])
        ih[...] = high
        il[...] = low

    for c in range(chunks):
        b_copies[c].wait()
        y_make(0, c)

    lags = [0] * panels
    for k in range(1, panels):
        lags[k] = 2 * k
    steps = chunks + 2 * (panels - 1)
    per_step = -(-len(ups) // steps)
    early, late = set(), set()
    for t in range(steps):
        for _ in range(per_step):
            l_step()
        for k in range(panels):
            c = t - 2 * k
            if 0 <= c < chunks:
                y_recv(k, c)
            if k + 1 < panels:
                c -= 1
                todo = [c] if 0 <= c < chunks else []
                for c in todo:
                    l_need(k, lead)
                    y_lead(k, c)
                    y_make(k + 1, c)
        if len(seen_up) == len(ups) or t >= steps - 3:
            l_convert()
        ready = [p for p in range(panels - 1) if all((p, zz) in converted for zz in range(Z))]
        if len(ready) == panels - 1:
            budget = 0
            for c in range(chunks):
                if c <= t - 2 * (panels - 2) and c not in early and budget < 2:
                    early.add(c)
                    budget += 1
                    rest(tuple(ready), c)
    while state["next"] < len(ups):
        l_step()
    l_convert()
    for c in range(chunks):
        if c not in early:
            rest(tuple(range(panels - 1)), c)
        y_lead(panels - 1, c)
        rest((panels - 1,), c)
        write(c)
    for copy in outs:
        copy.wait()
    for cond, make in pending:
        @pl.when(cond)
        def _(make=make):
            make().wait_send()


def local(R, S, right_side, lower_panels, inverse_blocks):
    rows, columns = right_side.shape
    panels, h, nb = lower_panels.shape
    chunks = columns // CHUNK
    share = panels * nb // R
    f32, bf16 = jnp.float32, jnp.bfloat16
    dma = pltpu.SemaphoreType.DMA
    anywhere = pl.BlockSpec(memory_space=pl.ANY)
    return pl.pallas_call(
        functools.partial(kernel, R, S),
        out_shape=(jax.ShapeDtypeStruct((share, columns), f32), jax.ShapeDtypeStruct((rows, columns), f32)),
        in_specs=[anywhere] * 3,
        out_specs=(anywhere, anywhere),
        scratch_shapes=[
            pltpu.VMEM((chunks, rows, CHUNK), f32),
            pltpu.VMEM((panels, S, h, nb), f32),
            pltpu.VMEM((panels, rows, nb), bf16),
            pltpu.VMEM((panels, rows, nb), bf16),
            pltpu.VMEM((panels, chunks, nb, CHUNK), f32),
            pltpu.VMEM((panels, chunks, nb, CHUNK), bf16),
            pltpu.VMEM((panels, chunks, nb, CHUNK), bf16),
            pltpu.VMEM((nb, nb), f32),
            pltpu.VMEM((nb, nb), bf16),
            pltpu.VMEM((nb, nb), bf16),
            dma((panels, S)),
            dma((3, panels, S)),
            dma((panels,)),
            dma((panels, chunks)),
            dma((2, panels, chunks)),
            dma((chunks,)),
            dma,
            dma((chunks,)),
            dma((share // math.gcd(share, nb), chunks)),
        ],
        compiler_params=pltpu.CompilerParams(
            collective_id=0, has_side_effects=True, vmem_limit_bytes=58 * 1024 * 1024
        ),
        cost_estimate=pl.CostEstimate(
            flops=6 * rows * panels * nb * columns, bytes_accessed=8 * rows * columns, transcendentals=0
        ),
    )(right_side, lower_panels, inverse_blocks)


def solution(mesh):
    placed = (P("row", "sim"), P(None, ("row", "sim"), None), P())
    return jax.shard_map(
        functools.partial(local, mesh.shape["row"], mesh.shape["sim"]),
        mesh=mesh,
        in_specs=placed,
        out_specs=(P("row", "sim"), P("row", "sim")),
        check_vma=False,
    )
```

```python
import functools
import heapq
import itertools
import math

import jax
import jax.numpy as jnp
from jax import lax
from jax.experimental import pallas as pl
from jax.experimental.pallas import tpu as pltpu
from jax.sharding import PartitionSpec as P

MESH = pl.DeviceIdType.MESH
CHUNK = 256
TILE = 256
PARTS = 2
HOP = 1.0
STEP = 1.5
L_TIME = 3.93
Y_TIME = 5.25


def split(x):
    high = x.astype(jnp.bfloat16)
    return high, (x - high.astype(jnp.float32)).astype(jnp.bfloat16)


def mul(a, b):
    return jnp.dot(a, b, preferred_element_type=jnp.float32)


def ring_position(row, rows):
    return row // 2 if row % 2 == 0 else rows - 1 - row // 2


def line_plan(Z, panels, halves, lead, nb, h, upward):
    free, pending = [0.0] * Z, [[] for _ in range(Z)]

    def rank(piece):
        p, zz, j = piece
        source = zz if upward else Z - 1 - zz
        first = p < panels - 1 and source < lead
        return (0, p, zz, j) if first else (1, p, -zz, j)

    for zz in range(Z - 1):
        pending[zz] = [(0.0, (p, zz, j)) for p in range(panels) for j in range(halves)]
    sends, arrivals = [], {}
    while any(pending):
        start, link = min((max(free[q], min(t for t, _ in pending[q])), q) for q in range(Z) if pending[q])
        ready = [entry for entry in pending[link] if entry[0] <= start]
        entry = min(ready, key=lambda e: rank(e[1]))
        pending[link].remove(entry)
        piece = entry[1]
        free[link] = start + L_TIME
        arrival = start + L_TIME + HOP
        real = (lambda q: q) if upward else (lambda q: Z - 1 - q)
        name = (piece[0], real(piece[1]), piece[2])
        sends.append((start if piece[1] == link else entry[0], real(link), name))
        arrivals[name, real(link + 1)] = arrival
        if link + 1 < Z - 1:
            pending[link + 1].append((arrival, piece))
    return sends, arrivals


def ring_sim(R, panels, chunks, parts, lead_ready, reach):
    makes,leads,arr,got,sends={}, {}, {}, {}, []
    busy=[0.0]*panels
    links={}
    heap=[]; n=itertools.count()
    for c in range(chunks):
        makes[0,c]=0.5*c
        for g in range(parts): heapq.heappush(heap,(1+0.5*c+0.1*g,next(n),0,c,g,ring_position(0,R),0,0))
    nextc=[0]*panels
    free={}
    while heap:
        t,_,k,c,g,q,way,left=heapq.heappop(heap)
        if way:
            arr[k,c,g,q]=t
            if all((k,c,x,q) in arr for x in range(parts)): got[k,c,q]=t
        todo=[(way,left)] if way else [(1,reach(k,c,g)),(-1,R-1-reach(k,c,g))]
        for w,l in todo:
            if l>0:
                s=max(t,free.get((q,w),0)); free[q,w]=s+Y_TIME
                heapq.heappush(heap,(s+Y_TIME+HOP,next(n),k,c,g,(q+w)%R,w,l-1))
        for o in range(1,panels):
            p=ring_position(o,R)
            while nextc[o]<chunks and all((e,nextc[o],p) in got for e in range(o)):
                cc=nextc[o]; nextc[o]+=1
                done=busy[o]
                for e in range(o):
                    leads[o,e,cc]=max(done,got[e,cc,p]+0.2,lead_ready[e]); done=leads[o,e,cc]+STEP
                makes[o,cc]=done; busy[o]=done+STEP
                for g2 in range(parts): heapq.heappush(heap,(done+STEP*(g2+1)/parts,next(n),o,cc,g2,p,0,0))
    return arr,got,leads,makes
def kernel(R, S, b_hbm, l_hbm, inv_hbm, solved_hbm, upd_hbm, bv, lg, lh, ll, yv, yh, yl, iv, ih, il,
           lrecv, lsend, lown, yrecv, ysend, bsem, isem, osem, ssem):
    panels, chunks, nb, width = yv.shape
    rows = bv.shape[1]
    h = lg.shape[2]
    Z = S // 2
    sub, seg = h // PARTS, nb // PARTS
    r, s = lax.axis_index("row"), lax.axis_index("sim")
    z, core = s // 2, s % 2
    partner = s + 1 - 2 * core
    half = R // 2
    pos = jnp.where(r % 2 == 0, r // 2, R - 1 - r // 2)

    def row_at(position):
        q = lax.rem(position + R, R)
        return jnp.where(q < half, 2 * q, 2 * (R - 1 - q) + 1)

    right, left = row_at(pos + 1), row_at(pos - 1)
    up, down = lax.rem(s + 2, S), lax.rem(s + S - 2, S)

    barrier = pltpu.get_barrier_semaphore()
    for target in ((right, s), (left, s), (r, up), (r, down), (r, partner)):
        pl.semaphore_signal(barrier, inc=1, device_id=target, device_id_type=MESH)

    own_copies = [pltpu.make_async_copy(l_hbm.at[p], lg.at[p, s], lown.at[p]) for p in range(panels)]
    solver = r < panels
    inv_copy = pltpu.make_async_copy(inv_hbm.at[jnp.minimum(r, panels - 1)], iv, isem)
    inv_copy.start()
    b_copies = [
        pltpu.make_async_copy(b_hbm.at[:, pl.ds(c * width, width)], bv.at[c], bsem.at[c]) for c in range(chunks)
    ]
    b_copies[0].start()
    for copy in own_copies:
        copy.start()
    for copy in b_copies[1:]:
        copy.start()
    pl.semaphore_wait(barrier, 5)

    pending = []

    def send(cond, make):
        @pl.when(cond)
        def _():
            make().start()

        pending.append((cond, make))

    def l_copy(p, slot, j, way, target, own):
        src = l_hbm.at[p, pl.ds(j * sub, sub)] if own else lg.at[p, slot, pl.ds(j * sub, sub)]
        return pltpu.make_async_remote_copy(
            src_ref=src, dst_ref=lg.at[p, slot, pl.ds(j * sub, sub)], send_sem=lsend.at[way, p, slot, j],
            recv_sem=lrecv.at[p, slot, j], device_id=(r, target), device_id_type=MESH,
        )

    def l_send(zz, way, piece):
        p, source, j = piece
        slot, target = 2 * source + core, up if way == 0 else down
        send(z == zz, lambda: l_copy(p, slot, j, way, target, source == zz))

    def l_arrive(zz, piece):
        p, source, j = piece
        slot = 2 * source + core

        @pl.when(z == zz)
        def _():
            l_copy(p, slot, j, 0, up, False).wait_recv()

        send(z == zz, lambda: l_copy(p, slot, j, 2, partner, False))

    own_waited = set()

    def convert(p, zz):
        if p not in own_waited:
            own_waited.add(p)
            own_copies[p].wait()
        for j in range(PARTS):
            l_copy(p, 2 * zz + 1 - core, j, 2, partner, False).wait_recv()
        for k in range(2):
            first = (2 * zz + k) * h
            high, low = split(lg[p, 2 * zz + k])
            lh[p, first:first + h] = high
            ll[p, first:first + h] = low

    def y_copy(k, c, g, way, target):
        part = yv.at[k, c, pl.ds(g * seg, seg)]
        return pltpu.make_async_remote_copy(
            src_ref=part, dst_ref=part, send_sem=ysend.at[way, k, c, g], recv_sem=yrecv.at[k, c, g],
            device_id=(target, s), device_id_type=MESH,
        )

    def reach(k, c, g):
        index, total = c * PARTS + g, chunks * PARTS
        if k == 1:
            return R - 1 if 10 * index < 3 * total else half - 1
        return 0 if 10 * index < (4 if k == 0 else 6) * total else half

    def y_make(k, c):
        @pl.when(r == k)
        def _():
            high, low = split(bv[c, 0:nb])
            for g in range(PARTS):
                part = slice(g * seg, (g + 1) * seg)
                value = mul(ih[part], high) + mul(ih[part], low) + mul(il[part], high)
                yv[k, c, part] = value
                if reach(k, c, g) > 0:
                    y_copy(k, c, g, 0, right).start()
                if reach(k, c, g) < R - 1:
                    y_copy(k, c, g, 1, left).start()
                yh[k, c, part], yl[k, c, part] = split(value)

        for g in range(PARTS):
            if reach(k, c, g) > 0:
                pending.append((r == k, lambda g=g: y_copy(k, c, g, 0, right)))
            if reach(k, c, g) < R - 1:
                pending.append((r == k, lambda g=g: y_copy(k, c, g, 1, left)))

    def y_arrive(k, c, g, q):
        d = (q - ring_position(k, R)) % R
        rightward = reach(k, c, g)
        way = None
        if d < rightward:
            way = 0
        elif d > rightward and R - d < R - 1 - rightward:
            way = 1

        @pl.when(pos == q)
        def _():
            y_copy(k, c, g, 0, right).wait_recv()
            if way is not None:
                y_copy(k, c, g, way, (right, left)[way]).start()

        if way is not None:
            pending.append((pos == q, lambda: y_copy(k, c, g, way, (right, left)[way])))

    def y_split(k, c):
        @pl.when(r != k)
        def _():
            yh[k, c], yl[k, c] = split(yv[k, c])

    def update(ps, c, start, count):
        def body(i, carry):
            rows_i = pl.ds(pl.multiple_of(start + i * TILE, TILE), TILE)
            total = None
            for p in ps:
                part = mul(lh[p, rows_i], yh[p, c]) + mul(lh[p, rows_i], yl[p, c]) + mul(ll[p, rows_i], yh[p, c])
                total = part if total is None else total + part
            bv[c, rows_i] = bv[c, rows_i] - total
            return carry

        lax.fori_loop(0, count // TILE, body, 0)

    def y_lead(o, k, c):
        @pl.when(r == o)
        def _():
            yh[k, c], yl[k, c] = split(yv[k, c])
            update((k,), c, 0, nb)

    def rest(p, c):
        start = jnp.where(solver, nb, 0)
        update((p,), c, start, rows - start)

    outs = []

    def write(c):
        copy = pltpu.make_async_copy(bv.at[c], upd_hbm.at[:, pl.ds(c * width, width)], osem.at[c])
        copy.start()
        outs.append(copy)
        share = solved_hbm.shape[0]
        piece = math.gcd(share, nb)
        for i in range(share // piece):
            q = r * share + i * piece
            source = yv.at[q // nb, c, pl.ds(pl.multiple_of(q % nb, piece), piece)]
            copy = pltpu.make_async_copy(
                source, solved_hbm.at[pl.ds(i * piece, piece), pl.ds(c * width, width)], ssem.at[i, c]
            )
            copy.start()
            outs.append(copy)

    events = []

    def at(time, action, *args):
        events.append((time, len(events), action, args))

    lead = min(Z, -(-nb // (2 * h)))
    converted = {(p, zz): 1.5 for p in range(panels) for zz in range(Z)}
    for way in (0, 1):
        sends, arrivals = line_plan(Z, panels, PARTS, lead, nb, h, way == 0)
        for time, zz, piece in sends:
            own = piece[1] == zz
            at(max(time - 1.5 * L_TIME, -1.0 + 0.001 * time) if own else time + 0.2, l_send, zz, way, piece)
        for (piece, zz), time in arrivals.items():
            at(time + 0.1, l_arrive, zz, piece)
            converted[piece[:2]] = max(converted[piece[:2]], time + 1.5)
    for (p, zz), time in converted.items():
        at(time, convert, p, zz)
    ready = [max(converted[p, zz] for zz in range(lead)) + 0.1 for p in range(panels)]
    whole = [max(converted[p, zz] for zz in range(Z)) + 0.1 for p in range(panels)]
    arrivals, got, leads, makes = ring_sim(R, panels, chunks, PARTS, ready, reach)
    for (k, c), time in makes.items():
        at(time, y_make, k, c)
    for (k, c, g, q), time in arrivals.items():
        at(time, y_arrive, k, c, g, q)
    for (o, k, c), time in leads.items():
        at(time, y_lead, o, k, c)
    for c in range(chunks):
        last = 0.0
        for k in range(panels):
            present = max(time for (a, b, _), time in got.items() if (a, b) == (k, c)) + 0.3
            at(present, y_split, k, c)
            last = max(last, present + 0.1, whole[k] + 0.01 * c)
            at(max(present + 0.1, whole[k] + 0.01 * c), rest, k, c)
        at(last + 0.05, write, c)

    for p in range(panels):
        for j in range(PARTS):
            send(z >= 0, lambda p=p, j=j: l_copy(p, s, j, 2, partner, True))
    events.sort(key=lambda e: e[:2])
    for time, _, action, args in events:
        if time < 0.0:
            action(*args)
    inv_copy.wait()

    @pl.when(solver)
    def _():
        ih[...], il[...] = split(iv[...])

    for copy in b_copies:
        copy.wait()
    for time, _, action, args in events:
        if time >= 0.0:
            action(*args)
    for copy in outs:
        copy.wait()
    for cond, make in pending:
        @pl.when(cond)
        def _(make=make):
            make().wait_send()


def local(R, S, right_side, lower_panels, inverse_blocks):
    rows, columns = right_side.shape
    panels, h, nb = lower_panels.shape
    chunks = columns // CHUNK
    share = panels * nb // R
    f32, bf16 = jnp.float32, jnp.bfloat16
    dma = pltpu.SemaphoreType.DMA
    anywhere = pl.BlockSpec(memory_space=pl.ANY)
    return pl.pallas_call(
        functools.partial(kernel, R, S),
        out_shape=(jax.ShapeDtypeStruct((share, columns), f32), jax.ShapeDtypeStruct((rows, columns), f32)),
        in_specs=[anywhere] * 3,
        out_specs=(anywhere, anywhere),
        scratch_shapes=[
            pltpu.VMEM((chunks, rows, CHUNK), f32),
            pltpu.VMEM((panels, S, h, nb), f32),
            pltpu.VMEM((panels, rows, nb), bf16),
            pltpu.VMEM((panels, rows, nb), bf16),
            pltpu.VMEM((panels, chunks, nb, CHUNK), f32),
            pltpu.VMEM((panels, chunks, nb, CHUNK), bf16),
            pltpu.VMEM((panels, chunks, nb, CHUNK), bf16),
            pltpu.VMEM((nb, nb), f32),
            pltpu.VMEM((nb, nb), bf16),
            pltpu.VMEM((nb, nb), bf16),
            dma((panels, S, PARTS)),
            dma((3, panels, S, PARTS)),
            dma((panels,)),
            dma((panels, chunks, PARTS)),
            dma((2, panels, chunks, PARTS)),
            dma((chunks,)),
            dma,
            dma((chunks,)),
            dma((share // math.gcd(share, nb), chunks)),
        ],
        compiler_params=pltpu.CompilerParams(
            collective_id=0, has_side_effects=True, vmem_limit_bytes=58 * 1024 * 1024
        ),
        cost_estimate=pl.CostEstimate(
            flops=6 * rows * panels * nb * columns, bytes_accessed=8 * rows * columns, transcendentals=0
        ),
    )(right_side, lower_panels, inverse_blocks)


def solution(mesh):
    placed = (P("row", "sim"), P(None, ("row", "sim"), None), P())
    return jax.shard_map(
        functools.partial(local, mesh.shape["row"], mesh.shape["sim"]),
        mesh=mesh,
        in_specs=placed,
        out_specs=(P("row", "sim"), P("row", "sim")),
        check_vma=False,
    )
```
